256 devices in a mesh: tok: 64 (over z_lo, y, x), hid: 4 (over z_hi, core).
Axes of the slice: x: 4, y: 4, z: 8 (z_hi: 2, z_lo: 4; z = z_hi * 4 + z_lo), core: 2. Of those that a mesh axis runs over, the one named last changes fastest.
Arguments:
- train_grads: bfloat16 [32768, 28672], P('tok', 'hid'), may hold values from -6 to 6
- train_acts: bfloat16 [32768, 8192], P('tok', 'hid'), may hold values from -6 to 6
- out_factors: bfloat16 [28672, 1024], P('hid', 'tok'), may hold values from -0.03125 to 0.03125
- in_factors: bfloat16 [8192, 1024], P('hid', 'tok'), may hold values from -0.0625 to 0.0625
Outputs:
- scores: float32 [512, 128], P('tok', 'hid')
The draws below stay inside these ranges and needn't reach their ends.
All inputs are finite; a program needn't handle non-finite values.
Results may differ from the reference program's by a relative error of at most 0.0003.
Values may be sent and summed in bfloat16 or wider, within the bound.
No kernel may reach another device: no remote copies, remote signals or barrier semaphores. Data moves between devices by JAX's collectives and lax.ppermute only.
A program may use at most 128 MiB of HBM per device.

```python
import math
import jax
import jax.numpy as jnp
from jax import lax

D_IN = 8192
D_OUT = 28672
RANK = 8
SEQ_LEN = 64
QUERIES = 128
SEQS = 512
TOKENS = 32768
COLS = 1024


def block_levels(own_key, dims, cuts, least, largest):
    gain = 1.0
    for axis_at, shards_of in cuts:
        heights = jax.random.uniform(jax.random.fold_in(jax.random.fold_in(own_key, 6), axis_at), (shards_of,), jnp.float32, least / len(cuts), largest / len(cuts))
        gain = gain * jnp.repeat(jnp.exp(heights), dims[axis_at] // shards_of).reshape((-1,) + (1,) * (len(dims) - 1 - axis_at))
    return gain


def scatter_about(rng, extent, width, bound, pieces=(), held_as=jnp.bfloat16):
    array = width * jax.random.normal(rng, extent, jnp.float32)
    if pieces:
        array = array * block_levels(rng, extent, pieces, -0.22, 0.18)
    return jnp.clip(array, -bound, bound).astype(held_as)


def setup_inputs(seed: int = 0) -> dict:
    splits = jax.random.split(jax.random.key(seed), 5)
    train_grads = scatter_about(splits[0], (TOKENS, D_OUT), 1.0, 6.0, ((0, 64), (1, 4)))
    train_acts = scatter_about(splits[1], (TOKENS, D_IN), 1.0, 6.0, ((0, 64), (1, 4)))
    out_factors = scatter_about(splits[2], (D_OUT, COLS), D_OUT ** -0.5, 0.03125, ((0, 4), (1, 64)))
    in_factors = scatter_about(splits[3], (D_IN, COLS), D_IN ** -0.5, 0.0625, ((0, 4), (1, 64)))
    return dict(train_grads=train_grads, train_acts=train_acts, out_factors=out_factors, in_factors=in_factors)


def reference(train_grads, train_acts, out_factors, in_factors):
    group = math.gcd(SEQS, 8)
    rows = group * SEQ_LEN
    out_wide = out_factors.astype(jnp.float32)
    in_wide = in_factors.astype(jnp.float32)
    grad_blocks = train_grads.reshape(SEQS // group, rows, D_OUT)
    act_blocks = train_acts.reshape(SEQS // group, rows, D_IN)
    scale = 1.0 / math.sqrt(SEQ_LEN * RANK)

    def block_scores(pair):
        grad_rows, act_rows = pair
        grad_proj = jnp.dot(grad_rows.astype(jnp.float32), out_wide, preferred_element_type=jnp.float32, precision=lax.Precision.HIGHEST)
        act_proj = jnp.dot(act_rows.astype(jnp.float32), in_wide, preferred_element_type=jnp.float32, precision=lax.Precision.HIGHEST)
        joined = (grad_proj * act_proj).reshape(group, SEQ_LEN, QUERIES, RANK)
        return lax.optimization_barrier(jnp.sum(joined, axis=(1, 3))) * scale
    result = lax.map(block_scores, (grad_blocks, act_blocks))
    return result.reshape(SEQS, QUERIES)
```

```python
import math

import jax
import jax.numpy as jnp
from jax import lax
from jax.sharding import Mesh, PartitionSpec as P

RANK = 8
SEQ_LEN = 64
AXES = ("zl", "y", "x", "zh", "core")
SIZES = (4, 4, 4, 2, 2)


def ring(x, axis, step):
    n = SIZES[AXES.index(axis)]
    return lax.ppermute(x, axis, [(i, (i + step) % n) for i in range(n)])


def both_ways(block, axis):
    half = block.shape[0] // 2
    before = ring(block, axis, 1)
    after = ring(block, axis, -1)
    far = (ring(before[:half], axis, 1), ring(after[half:], axis, -1))
    return before, after, far


def project(rows, grads, acts):
    cut = grads.shape[1]
    dims = (((1,), (1,)), ((), ()))
    return (
        lax.dot_general(rows[:, :cut], grads, dims, preferred_element_type=jnp.float32),
        lax.dot_general(rows[:, cut:], acts, dims, preferred_element_type=jnp.float32),
    )


def shards(train_grads, train_acts, out_factors, in_factors):
    zl, y, x = (lax.axis_index(a) for a in ("zl", "y", "x"))
    zh, core = lax.axis_index("zh"), lax.axis_index("core")
    tokens = train_grads.shape[0]
    own = jnp.concatenate([out_factors.T, in_factors.T], axis=1)
    features = own.shape[1]

    with jax.named_scope("z_shifts"):
        shifted = jnp.stack([own] + [ring(own, "zl", d) for d in (1, 2, 3)])
        order = [(zl - 2 * (zh ^ (j & 1)) - (core ^ (j >> 1))) % 4 for j in range(4)]
        placed = jnp.concatenate(
            [lax.dynamic_slice_in_dim(shifted, d, 1, 0) for d in order]
        )

    def flat(blocks):
        return jnp.concatenate(blocks)

    phase = {}
    with jax.named_scope("first_axis"):
        for name, axis, rows in (
            ("a", "y", placed[:, :RANK]),
            ("b", "x", placed[:, RANK:]),
        ):
            block = rows.reshape(4 * RANK, features)
            before, after, far = both_ways(block, axis)
            phase[name] = flat([block, before, after, far[0], far[1]])
    with jax.named_scope("second_axis"):
        last = {
            name: both_ways(phase[name], axis) for name, axis in (("a", "x"), ("b", "y"))
        }

    def reduce(blocks):
        parts = []
        for block in blocks:
            for p in project(block, train_grads, train_acts):
                parts.append(p.reshape(-1, 2, 2, RANK, tokens))
        joined = jnp.concatenate(parts)
        got = lax.ppermute(joined[:, 1], "core", [(0, 1), (1, 0)])
        mine = joined[:, 0] + got
        total = mine[:, 0] + lax.ppermute(mine[:, 1], "zh", [(0, 1), (1, 0)])
        out = []
        at = 0
        for block in blocks:
            n = block.shape[0] // (4 * RANK)
            out.append((total[at : at + n] * total[at + n : at + 2 * n]).sum(axis=1))
            at += 2 * n
        return out

    with jax.named_scope("reduce"):
        a0, b0 = reduce([phase["a"], phase["b"]])
        a1, a2, b1, b2 = reduce([last["a"][0], last["a"][1], last["b"][0], last["b"][1]])
        far = [jnp.concatenate(last[name][2]) for name in ("a", "b")]
        a3, b3 = reduce(far)
        every = jnp.concatenate([a0, a1, a2, a3, b0, b1, b2, b3])
        sums = every.reshape(32, tokens // SEQ_LEN, SEQ_LEN).sum(axis=2)

    with jax.named_scope("order"):
        steps = jnp.array([0, -1, 1, 2])
        here = jnp.arange(32)
        colour, second, first = here // 16, steps[(here // 4) % 4], steps[here % 4]
        at_y = (y + jnp.where(colour == 0, first, second)) % 4
        at_x = (x + jnp.where(colour == 0, second, first)) % 4
        target = (at_y * 4 + at_x) * 2 + colour
        pick = target[:, None] == jnp.arange(32)[None, :]
        scale = 1.0 / math.sqrt(SEQ_LEN * RANK)
        return jnp.where(pick[:, None, :], sums[:, :, None], 0.0).sum(axis=0) * scale


def solution(mesh):
    fine = Mesh(mesh.devices.reshape(SIZES), AXES)
    tok, hid = ("zl", "y", "x"), ("zh", "core")
    return jax.shard_map(
        shards,
        mesh=fine,
        in_specs=(P(tok, hid), P(tok, hid), P(hid, tok), P(hid, tok)),
        out_specs=P(tok, hid),
        check_vma=False,
    )
```

```python
import functools
import math

import jax
import jax.numpy as jnp
from jax import lax
from jax.experimental import pallas as pl
from jax.experimental.pallas import tpu as pltpu
from jax.sharding import Mesh, PartitionSpec as P

RANK = 8
SEQ_LEN = 64
AXES = ("zl", "y", "x", "zh", "core")
SIZES = (4, 4, 4, 2, 2)
DEPTH = 1024
VMEM_LIMIT = 20 << 20
SLOTS = 3


def ring(x, axis, step):
    n = SIZES[AXES.index(axis)]
    return lax.ppermute(x, axis, [(i, (i + step) % n) for i in range(n)])


def flip(x, axis, mask):
    n = SIZES[AXES.index(axis)]
    return lax.ppermute(x, axis, [(i, i ^ mask) for i in range(n)])


def flip_hid(x, mask):
    return lax.ppermute(x, ("zh", "core"), [(i, i ^ mask) for i in range(4)])


def project_kernel(blocks, grad_steps, place_ref, *refs):
    rows_refs = refs[:blocks]
    grads_ref, acts_ref, keep_ref, send_ref, total_ref, held_ref, sems = refs[blocks:]
    step, steps = pl.program_id(0), pl.num_programs(0)

    def copy(source, at):
        depth = held_ref.shape[2]
        start = at * depth
        if not isinstance(start, int):
            start = pl.multiple_of(start, depth)
        return source.at[:, pl.ds(start, depth)]

    def fetch(at):
        slot = lax.rem(at, SLOTS)

        @pl.when(at < grad_steps)
        def _():
            pltpu.make_async_copy(copy(grads_ref, at), held_ref.at[slot], sems.at[slot]).start()

        @pl.when(at >= grad_steps)
        def _():
            pltpu.make_async_copy(
                copy(acts_ref, at - grad_steps), held_ref.at[slot], sems.at[slot]
            ).start()

    @pl.when(step == 0)
    def _():
        total_ref[...] = jnp.zeros_like(total_ref)
        for at in range(SLOTS - 1):
            fetch(jnp.int32(at))

    @pl.when(step + SLOTS - 1 < steps)
    def _():
        fetch(step + SLOTS - 1)

    slot = lax.rem(step, SLOTS)
    pltpu.make_async_copy(copy(acts_ref, 0), held_ref.at[slot], sems.at[slot]).wait()
    rows = jnp.concatenate([r[...] for r in rows_refs], axis=0)
    part = jnp.where(step < grad_steps, 0, 1)
    total_ref[part] += lax.dot_general(
        rows, held_ref[slot], (((1,), (1,)), ((), ())), preferred_element_type=jnp.float32
    )

    @pl.when(step == steps - 1)
    def _():
        quarter = total_ref.shape[2] // 4
        zh, core = place_ref[0], place_ref[1]
        for to, ref in ((core, keep_ref), (1 - core, send_ref)):
            for other in range(2):
                at = (2 * to + (zh ^ other)) * quarter
                ref[other] = total_ref[:, :, pl.ds(pl.multiple_of(at, quarter), quarter)]


def project(blocks, grads, acts, place):
    tokens = grads.shape[0]
    grad_steps, act_steps = grads.shape[1] // DEPTH, acts.shape[1] // DEPTH
    rows = sum(b.shape[0] for b in blocks)
    half = jax.ShapeDtypeStruct((2, 2, rows, tokens // 4), jnp.float32)
    return pl.pallas_call(
        functools.partial(project_kernel, len(blocks), grad_steps),
        out_shape=(half, half),
        grid_spec=pltpu.PrefetchScalarGridSpec(
            num_scalar_prefetch=1,
            grid=(grad_steps + act_steps,),
            in_specs=[pl.BlockSpec((b.shape[0], DEPTH), lambda k, p: (0, k)) for b in blocks]
            + [pl.BlockSpec(memory_space=pltpu.HBM)] * 2,
            out_specs=(pl.BlockSpec(half.shape, lambda k, p: (0, 0, 0, 0)),) * 2,
            scratch_shapes=[
                pltpu.VMEM((2, rows, tokens), jnp.float32),
                pltpu.VMEM((SLOTS, tokens, DEPTH), jnp.bfloat16),
                pltpu.SemaphoreType.DMA((SLOTS,)),
            ],
        ),
        compiler_params=pltpu.CompilerParams(vmem_limit_bytes=VMEM_LIMIT),
        cost_estimate=pl.CostEstimate(flops=1 << 20, bytes_accessed=1 << 16, transcendentals=0),
    )(place, *blocks, grads, acts)


def pick_kernel(place_ref, sums1_ref, sums2_ref, kept_ref, got_ref, back_ref, out_ref):
    zh, core, zl, y, x = (place_ref[i] for i in range(5))
    total = kept_ref[0] + got_ref[0] + back_ref[...]
    product = total[0] * total[1]
    sums3 = product.reshape(-1, RANK, product.shape[-1]).sum(axis=1)
    sums = jnp.concatenate([sums1_ref[...], sums2_ref[...], sums3], axis=0)
    row = lax.broadcasted_iota(jnp.int32, (128, 128), 0)
    column = lax.broadcasted_iota(jnp.int32, (128, 128), 1)
    mask, query = row // 32, row % 32
    group = zl ^ (2 * zh + core) ^ mask
    colour = query % 2
    off_y, off_x = (query // 8 - y) & 3, ((query // 2) % 4 - x) & 3

    def place(off):
        return jnp.where(off == 3, 1, jnp.where(off == 0, 0, off + 1))

    first = place(jnp.where(colour == 0, off_y, off_x))
    second = place(jnp.where(colour == 0, off_x, off_y))
    inner = first * 3 + group - 1
    source = jnp.where(
        second == 0,
        32 + colour * 12,
        jnp.where(second == 3, 104 + colour * 12, 56 + colour * 24 + (second - 1) * 12),
    )
    source = jnp.where(group == 0, query, source + inner)
    out = jnp.dot(
        (source == column).astype(jnp.float32),
        sums,
        precision=lax.Precision.HIGHEST,
        preferred_element_type=jnp.float32,
    )
    for m in range(4):
        out_ref[m] = out[32 * m : 32 * m + 32]


def pick(place, sums1, sums2, kept, got, back):
    return pl.pallas_call(
        pick_kernel,
        out_shape=jax.ShapeDtypeStruct((4, 32, 128), jnp.float32),
        in_specs=[pl.BlockSpec(memory_space=pltpu.SMEM)] + [pl.BlockSpec(memory_space=pltpu.VMEM)] * 5,
        out_specs=pl.BlockSpec(memory_space=pltpu.VMEM),
        compiler_params=pltpu.CompilerParams(vmem_limit_bytes=4 << 20),
    )(place, sums1, sums2, kept, got, back)


def finish_kernel(place_ref, *refs):
    parts, out_ref = refs[:4], refs[4]
    zh, core = place_ref[0], place_ref[1]
    row = lax.broadcasted_iota(jnp.int32, (8, 128), 0)
    token = lax.broadcasted_iota(jnp.int32, (8, 128), 1)
    total = jnp.zeros(out_ref.shape, jnp.float32)
    for m, part in enumerate(parts):
        quarter = 2 * (core ^ (m & 1)) + (zh ^ (m >> 1))
        ones = (row == 2 * quarter + token // SEQ_LEN).astype(jnp.float32)
        total += lax.dot_general(
            ones,
            part[...],
            (((1,), (1,)), ((), ())),
            precision=lax.Precision.HIGHEST,
            preferred_element_type=jnp.float32,
        )
    out_ref[...] = total * (1.0 / math.sqrt(SEQ_LEN * RANK))


def finish(place, parts):
    return pl.pallas_call(
        finish_kernel,
        out_shape=jax.ShapeDtypeStruct((8, 32), jnp.float32),
        in_specs=[pl.BlockSpec(memory_space=pltpu.SMEM)] + [pl.BlockSpec(memory_space=pltpu.VMEM)] * 4,
        out_specs=pl.BlockSpec(memory_space=pltpu.VMEM),
        compiler_params=pltpu.CompilerParams(vmem_limit_bytes=4 << 20),
    )(place, *parts)


def shards(train_grads, train_acts, out_factors, in_factors):
    place = jnp.stack([lax.axis_index(a) for a in ("zh", "core", "zl", "y", "x")])
    own = jnp.concatenate([out_factors.T, in_factors.T], axis=1)
    features = own.shape[1]
    wide = 3 * RANK

    with jax.named_scope("own_columns"):
        near = lax.all_gather(own, ("y", "x"), axis=0, tiled=True)

    with jax.named_scope("z_shifts"):
        shifted = jnp.stack([flip(own, "zl", k) for k in (1, 2, 3)])

    def first(rows, axis):
        block = rows.reshape(wide, features)
        return jnp.concatenate([block] + [ring(block, axis, s) for s in (1, -1, 2)])

    def halves(before, after):
        half = before.shape[0] // 2
        return before[:half], after[half:]

    def exchange(sent):
        return lax.ppermute(sent, "zh", [(0, 1), (1, 0)])

    def over(send):
        return lax.ppermute(send, "core", [(0, 1), (1, 0)])

    def sums(keep, got, back):
        total = keep[0] + got[0] + back
        return (total[0] * total[1]).reshape(-1, RANK, total.shape[-1]).sum(axis=1)

    with jax.named_scope("first_axis"):
        col_a = first(shifted[:, :RANK], "y")
        col_b = first(shifted[:, RANK:], "x")
        col_a, col_b = lax.optimization_barrier((col_a, col_b))
    with jax.named_scope("second_axis"):
        next_a = ring(col_a, "x", 1), ring(col_a, "x", -1)
        next_b = ring(col_b, "y", 1), ring(col_b, "y", -1)
    with jax.named_scope("reduce"):
        keep1, send1 = project((near, col_a, col_b), train_grads, train_acts, place)
        got1 = over(send1)
        next_a, next_b, keep1 = lax.optimization_barrier((next_a, next_b, keep1))
    with jax.named_scope("second_axis"):
        half_a, half_b = lax.optimization_barrier((halves(*next_a), halves(*next_b)))
        far_a = ring(half_a[0], "x", 1), ring(half_a[1], "x", -1)
        far_b = ring(half_b[0], "y", 1), ring(half_b[1], "y", -1)
    with jax.named_scope("reduce"):
        sums1 = sums(keep1, got1, exchange(keep1[1] + got1[1]))
        keep2, send2 = project(next_a + next_b, train_grads, train_acts, place)
        got2 = over(send2)
        sent2 = keep2[1] + got2[1]
        back2 = exchange(sent2)
        far_a, far_b, sums1 = lax.optimization_barrier((far_a, far_b, sums1))
        keep3, send3 = project(far_a + far_b, train_grads, train_acts, place)
        got3 = over(send3)
        sums2 = sums(keep2, got2, back2)
        back3 = exchange(keep3[1] + got3[1])
    with jax.named_scope("order"):
        parts = pick(place, sums1, sums2, keep3, got3, back3)
        parts = [parts[0]] + [flip_hid(parts[m], m) for m in (1, 2, 3)]
        return finish(place, parts)


def solution(mesh):
    fine = Mesh(mesh.devices.reshape(SIZES), AXES)
    tok, hid = ("zl", "y", "x"), ("zh", "core")
    return jax.shard_map(
        shards,
        mesh=fine,
        in_specs=(P(tok, hid), P(tok, hid), P(hid, tok), P(hid, tok)),
        out_specs=P(tok, hid),
        check_vma=False,
    )
```

```python
import functools
import math

import jax
import jax.numpy as jnp
from jax import lax
from jax.experimental import pallas as pl
from jax.experimental.pallas import tpu as pltpu
from jax.sharding import Mesh, PartitionSpec as P

RANK = 8
SEQ_LEN = 64
AXES = ("zl", "y", "x", "zh", "core")
SIZES = (4, 4, 4, 2, 2)
DEPTH = 1024
GROUPS = 4


def ring(x, axis, step):
    n = SIZES[AXES.index(axis)]
    return lax.ppermute(x, axis, [(i, (i + step) % n) for i in range(n)])


def flip(x, axis, mask):
    n = SIZES[AXES.index(axis)]
    return lax.ppermute(x, axis, [(i, i ^ mask) for i in range(n)])


def project_kernel(count, place_ref, *refs):
    rows_refs = refs[:count]
    grads_ref, acts_ref, keep_ref, send_ref, total_ref = refs[count:]
    tokens = grads_ref.shape[0]
    shape = (-1, GROUPS, RANK, tokens)
    start = 0
    for part, source in enumerate((grads_ref, acts_ref)):
        for at in range(0, source.shape[1], DEPTH):
            rows = jnp.concatenate([r[:, start : start + DEPTH] for r in rows_refs], axis=0)
            product = lax.dot_general(
                rows,
                source[:, at : at + DEPTH],
                (((1,), (1,)), ((), ())),
                preferred_element_type=jnp.float32,
            ).reshape(shape)
            total_ref[part] = product if at == 0 else total_ref[part] + product
            start += DEPTH
    base = place_ref[0]
    for other in range(2):
        mine = base ^ (2 * other)
        keep_ref[other] = total_ref[:, :, mine]
        send_ref[other] = total_ref[:, :, mine ^ 1]


def project(blocks, grads, acts, place):
    tokens, features = grads.shape[0], grads.shape[1] + acts.shape[1]
    rows = sum(b.shape[0] for b in blocks)
    parts = rows // (GROUPS * RANK)
    half = jax.ShapeDtypeStruct((2, 2, parts, RANK, tokens), jnp.float32)
    vmem = pl.BlockSpec(memory_space=pltpu.VMEM)
    return pl.pallas_call(
        functools.partial(project_kernel, len(blocks)),
        out_shape=(half, half),
        in_specs=[pl.BlockSpec(memory_space=pltpu.SMEM)] + [vmem] * (len(blocks) + 2),
        out_specs=(vmem, vmem),
        scratch_shapes=[pltpu.VMEM((2, parts, GROUPS, RANK, tokens), jnp.float32)],
        compiler_params=pltpu.CompilerParams(vmem_limit_bytes=VMEM_LIMIT),
        cost_estimate=pl.CostEstimate(flops=1 << 20, bytes_accessed=1 << 16, transcendentals=0),
    )(place, *blocks, grads, acts)


VMEM_LIMIT = 12 << 20


def finish_kernel(place_ref, sums1_ref, sums2_ref, kept_ref, got_ref, back_ref, out_ref):
    y, x = place_ref[1], place_ref[2]
    total = kept_ref[0] + got_ref[0] + back_ref[...]
    sums3 = (total[0] * total[1]).sum(axis=1)
    sums = jnp.concatenate([sums1_ref[...], sums2_ref[...], sums3], axis=0)
    seqs, tokens = out_ref.shape[0], sums.shape[1]
    row = lax.broadcasted_iota(jnp.int32, (seqs, tokens), 0)
    token = lax.broadcasted_iota(jnp.int32, (seqs, tokens), 1)
    ones = (row == token // SEQ_LEN).astype(jnp.float32)
    scores = lax.dot_general(
        ones,
        sums,
        (((1,), (1,)), ((), ())),
        precision=lax.Precision.HIGHEST,
        preferred_element_type=jnp.float32,
    )
    source = lax.broadcasted_iota(jnp.int32, (32, 32), 0)
    query = lax.broadcasted_iota(jnp.int32, (32, 32), 1)
    colour = query % 2
    off_y, off_x = (query // 8 - y) & 3, ((query // 2) % 4 - x) & 3

    def stands(off):
        return jnp.where(off == 3, 1, jnp.where(off == 0, 0, off + 1))

    first = stands(jnp.where(colour == 0, off_y, off_x))
    second = stands(jnp.where(colour == 0, off_x, off_y))
    wanted = first + jnp.where(
        second == 0,
        colour * 4,
        jnp.where(second == 3, 24 + colour * 4, 8 + colour * 8 + (second - 1) * 4),
    )
    out = jnp.dot(
        scores,
        (source == wanted).astype(jnp.float32),
        precision=lax.Precision.HIGHEST,
        preferred_element_type=jnp.float32,
    )
    out_ref[...] = out * (1.0 / math.sqrt(SEQ_LEN * RANK))


def finish(place, sums1, sums2, kept, got, back):
    vmem = pl.BlockSpec(memory_space=pltpu.VMEM)
    return pl.pallas_call(
        finish_kernel,
        out_shape=jax.ShapeDtypeStruct((8, 32), jnp.float32),
        in_specs=[pl.BlockSpec(memory_space=pltpu.SMEM)] + [vmem] * 5,
        out_specs=vmem,
        compiler_params=pltpu.CompilerParams(vmem_limit_bytes=4 << 20),
    )(place, sums1, sums2, kept, got, back)


def shards(train_grads, train_acts, out_factors, in_factors):
    zl, y, x, zh, core = (lax.axis_index(a) for a in AXES)
    place = jnp.stack([zl ^ (2 * zh + core), y, x])
    own = jnp.concatenate([out_factors.T, in_factors.T], axis=1)
    features = own.shape[1]

    with jax.named_scope("z_shifts"):
        stacked = jnp.stack([own] + [flip(own, "zl", k) for k in (1, 2, 3)])

    def first(rows, axis):
        block = rows.reshape(GROUPS * RANK, features)
        half = block.shape[0] // 2
        before, after = ring(block, axis, 1), ring(block, axis, -1)
        far = ring(before[:half], axis, 1), ring(after[half:], axis, -1)
        return jnp.concatenate([block, before, after, *far])

    def halves(before, after):
        half = before.shape[0] // 2
        return before[:half], after[half:]

    def exchange(sent):
        return lax.ppermute(sent, "zh", [(0, 1), (1, 0)])

    def over(send):
        return lax.ppermute(send, "core", [(0, 1), (1, 0)])

    def sums(keep, got, back):
        total = keep[0] + got[0] + back
        return (total[0] * total[1]).sum(axis=1)

    with jax.named_scope("first_axis"):
        col_a = first(stacked[:, :RANK], "y")
        col_b = first(stacked[:, RANK:], "x")
        col_a, col_b = lax.optimization_barrier((col_a, col_b))
    with jax.named_scope("second_axis"):
        next_a = ring(col_a, "x", 1), ring(col_a, "x", -1)
        next_b = ring(col_b, "y", 1), ring(col_b, "y", -1)
    with jax.named_scope("reduce"):
        keep1, send1 = project((col_a, col_b), train_grads, train_acts, place)
        got1 = over(send1)
        next_a, next_b, keep1 = lax.optimization_barrier((next_a, next_b, keep1))
    with jax.named_scope("second_axis"):
        half_a, half_b = lax.optimization_barrier((halves(*next_a), halves(*next_b)))
        far_a = ring(half_a[0], "x", 1), ring(half_a[1], "x", -1)
        far_b = ring(half_b[0], "y", 1), ring(half_b[1], "y", -1)
    with jax.named_scope("reduce"):
        sums1 = sums(keep1, got1, exchange(keep1[1] + got1[1]))
        keep2, send2 = project(next_a + next_b, train_grads, train_acts, place)
        got2 = over(send2)
        back2 = exchange(keep2[1] + got2[1])
        far_a, far_b, sums1 = lax.optimization_barrier((far_a, far_b, sums1))
        keep3, send3 = project(far_a + far_b, train_grads, train_acts, place)
        got3 = over(send3)
        sums2 = sums(keep2, got2, back2)
        back3 = exchange(keep3[1] + got3[1])
        return finish(place, sums1, sums2, keep3, got3, back3)


def solution(mesh):
    fine = Mesh(mesh.devices.reshape(SIZES), AXES)
    tok, hid = ("zl", "y", "x"), ("zh", "core")
    return jax.shard_map(
        shards,
        mesh=fine,
        in_specs=(P(tok, hid), P(tok, hid), P(hid, tok), P(hid, tok)),
        out_specs=P(tok, hid),
        check_vma=False,
    )
```

```python
import functools
import math

import jax
import jax.numpy as jnp
from jax import lax
from jax.experimental import pallas as pl
from jax.experimental.pallas import tpu as pltpu
from jax.sharding import Mesh, PartitionSpec as P

RANK = 8
SEQ_LEN = 64
AXES = ("zl", "y", "x", "zh", "core")
SIZES = (4, 4, 4, 2, 2)
DEPTH = 1024
GROUPS = 4


def ring(x, axis, step):
    n = SIZES[AXES.index(axis)]
    return lax.ppermute(x, axis, [(i, (i + step) % n) for i in range(n)])


def flip(x, axis, mask):
    n = SIZES[AXES.index(axis)]
    return lax.ppermute(x, axis, [(i, i ^ mask) for i in range(n)])


def project_kernel(count, place_ref, *refs):
    rows_refs = refs[:count]
    grads_ref, acts_ref, keep_ref, send_ref, total_ref = refs[count:]
    tokens = grads_ref.shape[0]
    shape = (-1, GROUPS, RANK, tokens)
    start = 0
    for part, source in enumerate((grads_ref, acts_ref)):
        for at in range(0, source.shape[1], DEPTH):
            rows = jnp.concatenate([r[:, start : start + DEPTH] for r in rows_refs], axis=0)
            product = lax.dot_general(
                rows,
                source[:, at : at + DEPTH],
                (((1,), (1,)), ((), ())),
                preferred_element_type=jnp.float32,
            ).reshape(shape)
            total_ref[part] = product if at == 0 else total_ref[part] + product
            start += DEPTH
    base = place_ref[0]
    for other in range(2):
        mine = base ^ (2 * other)
        keep_ref[other] = total_ref[:, :, mine]
        send_ref[other] = total_ref[:, :, mine ^ 1]


def project(blocks, grads, acts, place):
    tokens, features = grads.shape[0], grads.shape[1] + acts.shape[1]
    rows = sum(b.shape[0] for b in blocks)
    parts = rows // (GROUPS * RANK)
    half = jax.ShapeDtypeStruct((2, 2, parts, RANK, tokens), jnp.float32)
    vmem = pl.BlockSpec(memory_space=pltpu.VMEM)
    return pl.pallas_call(
        functools.partial(project_kernel, len(blocks)),
        out_shape=(half, half),
        in_specs=[pl.BlockSpec(memory_space=pltpu.SMEM)] + [vmem] * (len(blocks) + 2),
        out_specs=(vmem, vmem),
        scratch_shapes=[pltpu.VMEM((2, parts, GROUPS, RANK, tokens), jnp.float32)],
        compiler_params=pltpu.CompilerParams(vmem_limit_bytes=VMEM_LIMIT),
        cost_estimate=pl.CostEstimate(flops=1 << 20, bytes_accessed=1 << 16, transcendentals=0),
    )(place, *blocks, grads, acts)


VMEM_LIMIT = 12 << 20


def finish_kernel(place_ref, sums1_ref, sums2_ref, sums3_ref, kept_ref, got_ref, back_ref, out_ref):
    y, x = place_ref[1], place_ref[2]
    total = kept_ref[0] + got_ref[0] + back_ref[...]
    sums4 = (total[0] * total[1]).sum(axis=1)
    sums = jnp.concatenate([sums1_ref[...], sums2_ref[...], sums3_ref[...], sums4], axis=0)
    seqs, tokens = out_ref.shape[0], sums.shape[1]
    row = lax.broadcasted_iota(jnp.int32, (seqs, tokens), 0)
    token = lax.broadcasted_iota(jnp.int32, (seqs, tokens), 1)
    ones = (row == token // SEQ_LEN).astype(jnp.float32)
    scores = lax.dot_general(
        ones,
        sums,
        (((1,), (1,)), ((), ())),
        precision=lax.Precision.HIGHEST,
        preferred_element_type=jnp.float32,
    )
    source = lax.broadcasted_iota(jnp.int32, (32, 32), 0)
    query = lax.broadcasted_iota(jnp.int32, (32, 32), 1)
    colour = query % 2
    off_y, off_x = (query // 8 - y) & 3, ((query // 2) % 4 - x) & 3

    def stands(off):
        return jnp.where(off == 3, 1, jnp.where(off == 0, 0, off + 1))

    first = stands(jnp.where(colour == 0, off_y, off_x))
    second = stands(jnp.where(colour == 0, off_x, off_y))
    wanted = colour * 4 + jnp.where(
        second == 0,
        first,
        jnp.where(second == 3, 24 + first, 8 + 8 * (first // 2) + 2 * (second - 1) + first % 2),
    )
    out = jnp.dot(
        scores,
        (source == wanted).astype(jnp.float32),
        precision=lax.Precision.HIGHEST,
        preferred_element_type=jnp.float32,
    )
    out_ref[...] = out * (1.0 / math.sqrt(SEQ_LEN * RANK))


def finish(place, sums, kept, got, back):
    vmem = pl.BlockSpec(memory_space=pltpu.VMEM)
    return pl.pallas_call(
        finish_kernel,
        out_shape=jax.ShapeDtypeStruct((8, 32), jnp.float32),
        in_specs=[pl.BlockSpec(memory_space=pltpu.SMEM)] + [vmem] * 6,
        out_specs=vmem,
        compiler_params=pltpu.CompilerParams(vmem_limit_bytes=4 << 20),
    )(place, *sums, kept, got, back)


def shards(train_grads, train_acts, out_factors, in_factors):
    zl, y, x, zh, core = (lax.axis_index(a) for a in AXES)
    place = jnp.stack([zl ^ (2 * zh + core), y, x])
    own = jnp.concatenate([out_factors.T, in_factors.T], axis=1)
    features = own.shape[1]

    with jax.named_scope("z_shifts"):
        stacked = jnp.stack([own] + [flip(own, "zl", k) for k in (1, 2, 3)])

    def first(rows, axis):
        block = rows.reshape(GROUPS * RANK, features)
        half = block.shape[0] // 2
        before, after = ring(block, axis, 1), ring(block, axis, -1)
        far = ring(before[:half], axis, 1), ring(after[half:], axis, -1)
        return jnp.concatenate([block, before]), jnp.concatenate([after, *far])

    def both(block, axis):
        return ring(block, axis, 1), ring(block, axis, -1)

    def exchange(sent):
        return lax.ppermute(sent, "zh", [(0, 1), (1, 0)])

    def over(send):
        return lax.ppermute(send, "core", [(0, 1), (1, 0)])

    def sums(keep, got, back):
        total = keep[0] + got[0] + back
        return (total[0] * total[1]).sum(axis=1)

    def work(blocks):
        keep, send = project(blocks, train_grads, train_acts, place)
        return keep, over(send)

    with jax.named_scope("first_axis"):
        lo_a, hi_a = first(stacked[:, :RANK], "y")
        lo_b, hi_b = first(stacked[:, RANK:], "x")
        lo_a, lo_b = lax.optimization_barrier((lo_a, lo_b))
        hi_a, hi_b = lax.optimization_barrier((hi_a, hi_b))
    with jax.named_scope("second_axis"):
        lo = both(lo_a, "x") + both(lo_b, "y")
        hi = both(hi_a, "x") + both(hi_b, "y")
    with jax.named_scope("reduce"):
        keep1, got1 = work((lo_a, hi_a, lo_b, hi_b))
        lo, keep1 = lax.optimization_barrier((lo, keep1))
        sums1 = sums(keep1, got1, exchange(keep1[1] + got1[1]))
        keep2, got2 = work(lo)
        hi, keep2 = lax.optimization_barrier((hi, keep2))
        sums2 = sums(keep2, got2, exchange(keep2[1] + got2[1]))
    with jax.named_scope("second_axis"):
        from_lo, from_hi = lax.optimization_barrier(((lo[0], lo[2]), (hi[1], hi[3])))
        far = (
            ring(from_lo[0], "x", 1),
            ring(from_hi[0], "x", -1),
            ring(from_lo[1], "y", 1),
            ring(from_hi[1], "y", -1),
        )
    with jax.named_scope("reduce"):
        keep3, got3 = work(hi)
        back3 = exchange(keep3[1] + got3[1])
        far, sums1, sums2 = lax.optimization_barrier((far, sums1, sums2))
        keep4, got4 = work(far)
        sums3 = sums(keep3, got3, back3)
        back4 = exchange(keep4[1] + got4[1])
        return finish(place, (sums1, sums2, sums3), keep4, got4, back4)


def solution(mesh):
    fine = Mesh(mesh.devices.reshape(SIZES), AXES)
    tok, hid = ("zl", "y", "x"), ("zh", "core")
    return jax.shard_map(
        shards,
        mesh=fine,
        in_specs=(P(tok, hid), P(tok, hid), P(hid, tok), P(hid, tok)),
        out_specs=P(tok, hid),
        check_vma=False,
    )
```

```python
import functools
import math

import jax
import jax.numpy as jnp
from jax import lax
from jax.experimental import pallas as pl
from jax.experimental.pallas import tpu as pltpu
from jax.sharding import Mesh, PartitionSpec as P

RANK = 8
SEQ_LEN = 64
AXES = ("zl", "y", "x", "zh", "core")
SIZES = (4, 4, 4, 2, 2)
DEPTH = 1024
GROUPS = 4


def ring(x, axis, step):
    n = SIZES[AXES.index(axis)]
    return lax.ppermute(x, axis, [(i, (i + step) % n) for i in range(n)])


def flip(x, axis, mask):
    n = SIZES[AXES.index(axis)]
    return lax.ppermute(x, axis, [(i, i ^ mask) for i in range(n)])


def project_kernel(count, place_ref, *refs):
    rows_refs = refs[:count]
    grads_ref, acts_ref, keep_ref, send_ref, total_ref = refs[count:]
    tokens = grads_ref.shape[0]
    shape = (-1, GROUPS, RANK, tokens)
    start = 0
    for part, source in enumerate((grads_ref, acts_ref)):
        for at in range(0, source.shape[1], DEPTH):
            rows = jnp.concatenate([r[:, start : start + DEPTH] for r in rows_refs], axis=0)
            product = lax.dot_general(
                rows,
                source[:, at : at + DEPTH],
                (((1,), (1,)), ((), ())),
                preferred_element_type=jnp.float32,
            ).reshape(shape)
            total_ref[part] = product if at == 0 else total_ref[part] + product
            start += DEPTH
    base = place_ref[0]
    for other in range(2):
        mine = base ^ (2 * other)
        keep_ref[other] = total_ref[:, :, mine]
        send_ref[other] = total_ref[:, :, mine ^ 1]


def project(blocks, grads, acts, place):
    tokens, features = grads.shape[0], grads.shape[1] + acts.shape[1]
    rows = sum(b.shape[0] for b in blocks)
    parts = rows // (GROUPS * RANK)
    half = jax.ShapeDtypeStruct((2, 2, parts, RANK, tokens), jnp.float32)
    vmem = pl.BlockSpec(memory_space=pltpu.VMEM)
    return pl.pallas_call(
        functools.partial(project_kernel, len(blocks)),
        out_shape=(half, half),
        in_specs=[pl.BlockSpec(memory_space=pltpu.SMEM)] + [vmem] * (len(blocks) + 2),
        out_specs=(vmem, vmem),
        scratch_shapes=[pltpu.VMEM((2, parts, GROUPS, RANK, tokens), jnp.float32)],
        compiler_params=pltpu.CompilerParams(vmem_limit_bytes=VMEM_LIMIT),
        cost_estimate=pl.CostEstimate(flops=1 << 20, bytes_accessed=1 << 16, transcendentals=0),
    )(place, *blocks, grads, acts)


VMEM_LIMIT = 12 << 20


def finish_kernel(place_ref, sums1_ref, sums2_ref, sums3_ref, kept_ref, got_ref, back_ref, out_ref):
    y, x = place_ref[1], place_ref[2]
    total = kept_ref[0] + got_ref[0] + back_ref[...]
    sums4 = (total[0] * total[1]).sum(axis=1)
    sums = jnp.concatenate([sums1_ref[...], sums2_ref[...], sums3_ref[...], sums4], axis=0)
    seqs, tokens = out_ref.shape[0], sums.shape[1]
    row = lax.broadcasted_iota(jnp.int32, (seqs, tokens), 0)
    token = lax.broadcasted_iota(jnp.int32, (seqs, tokens), 1)
    ones = (row == token // SEQ_LEN).astype(jnp.float32)
    scores = lax.dot_general(
        ones,
        sums,
        (((1,), (1,)), ((), ())),
        precision=lax.Precision.HIGHEST,
        preferred_element_type=jnp.float32,
    )
    source = lax.broadcasted_iota(jnp.int32, (32, 32), 0)
    query = lax.broadcasted_iota(jnp.int32, (32, 32), 1)
    colour = query % 2
    off_y, off_x = (query // 8 - y) & 3, ((query // 2) % 4 - x) & 3

    def stands(off):
        return jnp.where(off == 3, 1, jnp.where(off == 0, 0, off + 1))

    first = stands(jnp.where(colour == 0, off_y, off_x))
    second = stands(jnp.where(colour == 0, off_x, off_y))
    wanted = colour * 4 + jnp.where(
        second == 0,
        first,
        jnp.where(second == 3, 24 + first, 8 + 8 * (first // 2) + 2 * (second - 1) + first % 2),
    )
    out = jnp.dot(
        scores,
        (source == wanted).astype(jnp.float32),
        precision=lax.Precision.HIGHEST,
        preferred_element_type=jnp.float32,
    )
    out_ref[...] = out * (1.0 / math.sqrt(SEQ_LEN * RANK))


def finish(place, sums, kept, got, back):
    vmem = pl.BlockSpec(memory_space=pltpu.VMEM)
    return pl.pallas_call(
        finish_kernel,
        out_shape=jax.ShapeDtypeStruct((8, 32), jnp.float32),
        in_specs=[pl.BlockSpec(memory_space=pltpu.SMEM)] + [vmem] * 6,
        out_specs=vmem,
        compiler_params=pltpu.CompilerParams(vmem_limit_bytes=4 << 20),
    )(place, *sums, kept, got, back)


def shards(train_grads, train_acts, out_factors, in_factors):
    zl, y, x, zh, core = (lax.axis_index(a) for a in AXES)
    place = jnp.stack([zl ^ (2 * zh + core), y, x])
    own = jnp.concatenate([out_factors.T, in_factors.T], axis=1)
    features = own.shape[1]
    with jax.named_scope("z_shifts"):
        stacked = jnp.stack([own] + [flip(own, "zl", k) for k in (1, 2, 3)])

    def first(rows, axis):
        block = rows.reshape(GROUPS * RANK, features)
        half = block.shape[0] // 2
        before, after = ring(block, axis, 1), ring(block, axis, -1)
        far = ring(before[:half], axis, 1), ring(after[half:], axis, -1)
        return jnp.concatenate([block, before]), jnp.concatenate([after, *far])

    def both(block, axis):
        return ring(block, axis, 1), ring(block, axis, -1)

    def exchange(sent):
        return lax.ppermute(sent, "zh", [(0, 1), (1, 0)])

    def over(send):
        return lax.ppermute(send, "core", [(0, 1), (1, 0)])

    def sums(keep, got, back):
        total = keep[0] + got[0] + back
        return (total[0] * total[1]).sum(axis=1)

    def work(blocks):
        keep, send = project(blocks, train_grads, train_acts, place)
        return keep, over(send)
    with jax.named_scope("first_axis"):
        lo_a, hi_a = first(stacked[:, :RANK], "y")
        lo_b, hi_b = first(stacked[:, RANK:], "x")
        lo_a, lo_b = lax.optimization_barrier((lo_a, lo_b))
        hi_a, hi_b = lax.optimization_barrier((hi_a, hi_b))
    with jax.named_scope("second_axis"):
        lo = both(lo_a, "x") + both(lo_b, "y")
    with jax.named_scope("reduce"):
        keep1, got1 = work((lo_a, hi_a, lo_b, hi_b))
        hi_a, hi_b, keep1 = lax.optimization_barrier((hi_a, hi_b, keep1))
        sums1 = sums(keep1, got1, exchange(keep1[1] + got1[1]))
        lo, keep1 = lax.optimization_barrier((lo, keep1))
    with jax.named_scope("second_axis"):
        hi = both(hi_a, "x") + both(hi_b, "y")
    with jax.named_scope("reduce"):
        keep2, got2 = work(lo)
        hi, (keep2, sums1) = lax.optimization_barrier((hi, (keep2, sums1)))
        sums2 = sums(keep2, got2, exchange(keep2[1] + got2[1]))
    with jax.named_scope("second_axis"):
        from_lo, from_hi = lax.optimization_barrier(((lo[0], lo[2]), (hi[1], hi[3])))
        far = (
            ring(from_lo[0], "x", 1),
            ring(from_hi[0], "x", -1),
            ring(from_lo[1], "y", 1),
            ring(from_hi[1], "y", -1),
        )
    with jax.named_scope("reduce"):
        keep3, got3 = work(hi)
        sent3 = keep3[1] + got3[1]
        back3 = exchange(sent3)
        far, sums2, sent3 = lax.optimization_barrier((far, sums2, sent3))
        keep4, got4 = work(far)
        sums3 = sums(keep3, got3, back3)
        back4 = exchange(keep4[1] + got4[1])
        return finish(place, (sums1, sums2, sums3), keep4, got4, back4)


def solution(mesh):
    fine = Mesh(mesh.devices.reshape(SIZES), AXES)
    tok, hid = ("zl", "y", "x"), ("zh", "core")
    return jax.shard_map(
        shards,
        mesh=fine,
        in_specs=(P(tok, hid), P(tok, hid), P(hid, tok), P(hid, tok)),
        out_specs=P(tok, hid),
        check_vma=False,
    )
```

```python
import functools
import math

import jax
import jax.numpy as jnp
from jax import lax
from jax.experimental import pallas as pl
from jax.experimental.pallas import tpu as pltpu
from jax.sharding import Mesh, PartitionSpec as P

RANK = 8
SEQ_LEN = 64
AXES = ("zl", "y", "x", "zh", "core")
SIZES = (4, 4, 4, 2, 2)
DEPTH = 1024
GROUPS = 4


def ring(x, axis, step):
    n = SIZES[AXES.index(axis)]
    return lax.ppermute(x, axis, [(i, (i + step) % n) for i in range(n)])


def flip(x, axis, mask):
    n = SIZES[AXES.index(axis)]
    return lax.ppermute(x, axis, [(i, i ^ mask) for i in range(n)])


def project_kernel(count, place_ref, *refs):
    rows_refs = refs[:count]
    grads_ref, acts_ref, keep_ref, send_ref, total_ref = refs[count:]
    tokens = grads_ref.shape[0]
    shape = (-1, GROUPS, RANK, tokens)
    start = 0
    for part, source in enumerate((grads_ref, acts_ref)):
        for at in range(0, source.shape[1], DEPTH):
            rows = jnp.concatenate([r[:, start : start + DEPTH] for r in rows_refs], axis=0)
            product = lax.dot_general(
                rows,
                source[:, at : at + DEPTH],
                (((1,), (1,)), ((), ())),
                preferred_element_type=jnp.float32,
            ).reshape(shape)
            total_ref[part] = product if at == 0 else total_ref[part] + product
            start += DEPTH
    base = place_ref[0]
    for other in range(2):
        mine = base ^ (2 * other)
        keep_ref[other] = total_ref[:, :, mine]
        send_ref[other] = total_ref[:, :, mine ^ 1]


def project(blocks, grads, acts, place):
    tokens, features = grads.shape[0], grads.shape[1] + acts.shape[1]
    rows = sum(b.shape[0] for b in blocks)
    parts = rows // (GROUPS * RANK)
    half = jax.ShapeDtypeStruct((2, 2, parts, RANK, tokens), jnp.float32)
    vmem = pl.BlockSpec(memory_space=pltpu.VMEM)
    return pl.pallas_call(
        functools.partial(project_kernel, len(blocks)),
        out_shape=(half, half),
        in_specs=[pl.BlockSpec(memory_space=pltpu.SMEM)] + [vmem] * (len(blocks) + 2),
        out_specs=(vmem, vmem),
        scratch_shapes=[pltpu.VMEM((2, parts, GROUPS, RANK, tokens), jnp.float32)],
        compiler_params=pltpu.CompilerParams(vmem_limit_bytes=VMEM_LIMIT),
        cost_estimate=pl.CostEstimate(flops=1 << 20, bytes_accessed=1 << 16, transcendentals=0),
    )(place, *blocks, grads, acts)


VMEM_LIMIT = 12 << 20


def finish_kernel(place_ref, sums1_ref, sums2_ref, sums3_ref, kept_ref, got_ref, back_ref, out_ref):
    y, x = place_ref[1], place_ref[2]
    total = kept_ref[0] + got_ref[0] + back_ref[...]
    sums4 = (total[0] * total[1]).sum(axis=1)
    sums = jnp.concatenate([sums1_ref[...], sums2_ref[...], sums3_ref[...], sums4], axis=0)
    seqs, tokens = out_ref.shape[0], sums.shape[1]
    row = lax.broadcasted_iota(jnp.int32, (seqs, tokens), 0)
    token = lax.broadcasted_iota(jnp.int32, (seqs, tokens), 1)
    ones = (row == token // SEQ_LEN).astype(jnp.float32)
    scores = lax.dot_general(
        ones,
        sums,
        (((1,), (1,)), ((), ())),
        precision=lax.Precision.HIGHEST,
        preferred_element_type=jnp.float32,
    )
    source = lax.broadcasted_iota(jnp.int32, (32, 32), 0)
    query = lax.broadcasted_iota(jnp.int32, (32, 32), 1)
    colour = query % 2
    off_y, off_x = (query // 8 - y) & 3, ((query // 2) % 4 - x) & 3

    def stands(off):
        return jnp.where(off == 3, 1, jnp.where(off == 0, 0, off + 1))

    first = stands(jnp.where(colour == 0, off_y, off_x))
    second = stands(jnp.where(colour == 0, off_x, off_y))
    wanted = colour * 4 + jnp.where(
        second == 0,
        first,
        jnp.where(second == 3, 24 + first, 8 + 8 * (first // 2) + 2 * (second - 1) + first % 2),
    )
    out = jnp.dot(
        scores,
        (source == wanted).astype(jnp.float32),
        precision=lax.Precision.HIGHEST,
        preferred_element_type=jnp.float32,
    )
    out_ref[...] = out * (1.0 / math.sqrt(SEQ_LEN * RANK))


def finish(place, sums, kept, got, back):
    vmem = pl.BlockSpec(memory_space=pltpu.VMEM)
    return pl.pallas_call(
        finish_kernel,
        out_shape=jax.ShapeDtypeStruct((8, 32), jnp.float32),
        in_specs=[pl.BlockSpec(memory_space=pltpu.SMEM)] + [vmem] * 6,
        out_specs=vmem,
        compiler_params=pltpu.CompilerParams(vmem_limit_bytes=4 << 20),
    )(place, *sums, kept, got, back)


def shards(train_grads, train_acts, out_factors, in_factors):
    zl, y, x, zh, core = (lax.axis_index(a) for a in AXES)
    place = jnp.stack([zl ^ (2 * zh + core), y, x])
    own = jnp.concatenate([out_factors.T, in_factors.T], axis=1)
    features = own.shape[1]
    with jax.named_scope("z_shifts"):
        shifts = [own] + [flip(own, "zl", k) for k in (1, 2, 3)]
        pairs = [jnp.stack(shifts[k : k + 2]) for k in (0, 2)]
        pieces = [
            [p[:, at : at + RANK].reshape(2 * RANK, features) for p in pairs] for at in (0, RANK)
        ]

    def both(block, axis):
        return ring(block, axis, 1), ring(block, axis, -1)

    def exchange(sent):
        return lax.ppermute(sent, "zh", [(0, 1), (1, 0)])

    def over(send):
        return lax.ppermute(send, "core", [(0, 1), (1, 0)])

    def sums(keep, got, back):
        total = keep[0] + got[0] + back
        return (total[0] * total[1]).sum(axis=1)

    def work(blocks):
        keep, send = project(blocks, train_grads, train_acts, place)
        return keep, over(send)
    with jax.named_scope("first_axis"):
        (near_a, rest_a), (near_b, rest_b) = pieces
        around_a, around_b = both(near_a, "y"), both(near_b, "x")
        around_a, around_b, rest_a, rest_b = lax.optimization_barrier(
            (around_a, around_b, rest_a, rest_b)
        )
        beyond_a, beyond_b = both(rest_a, "y"), both(rest_b, "x")
        far_a = ring(around_a[0], "y", 1), ring(beyond_a[1], "y", -1)
        far_b = ring(around_b[0], "x", 1), ring(beyond_b[1], "x", -1)
        lo_a = jnp.concatenate([near_a, rest_a, around_a[0], beyond_a[0]])
        lo_b = jnp.concatenate([near_b, rest_b, around_b[0], beyond_b[0]])
        hi_a = jnp.concatenate([around_a[1], beyond_a[1], *far_a])
        hi_b = jnp.concatenate([around_b[1], beyond_b[1], *far_b])
        hi_a, hi_b = lax.optimization_barrier((hi_a, hi_b))
    with jax.named_scope("second_axis"):
        lo = both(lo_a, "x") + both(lo_b, "y")
    with jax.named_scope("reduce"):
        keep1, got1 = work((lo_a, hi_a, lo_b, hi_b))
        hi_a, hi_b, keep1 = lax.optimization_barrier((hi_a, hi_b, keep1))
        sums1 = sums(keep1, got1, exchange(keep1[1] + got1[1]))
        lo, keep1 = lax.optimization_barrier((lo, keep1))
    with jax.named_scope("second_axis"):
        hi = both(hi_a, "x") + both(hi_b, "y")
    with jax.named_scope("reduce"):
        keep2, got2 = work(lo)
        hi, (keep2, sums1) = lax.optimization_barrier((hi, (keep2, sums1)))
        sums2 = sums(keep2, got2, exchange(keep2[1] + got2[1]))
    with jax.named_scope("second_axis"):
        from_lo, from_hi = lax.optimization_barrier(((lo[0], lo[2]), (hi[1], hi[3])))
        far = (
            ring(from_lo[0], "x", 1),
            ring(from_hi[0], "x", -1),
            ring(from_lo[1], "y", 1),
            ring(from_hi[1], "y", -1),
        )
    with jax.named_scope("reduce"):
        keep3, got3 = work(hi)
        sent3 = keep3[1] + got3[1]
        back3 = exchange(sent3)
        far, sums2, sent3 = lax.optimization_barrier((far, sums2, sent3))
        keep4, got4 = work(far)
        sums3 = sums(keep3, got3, back3)
        back4 = exchange(keep4[1] + got4[1])
        return finish(place, (sums1, sums2, sums3), keep4, got4, back4)


def solution(mesh):
    fine = Mesh(mesh.devices.reshape(SIZES), AXES)
    tok, hid = ("zl", "y", "x"), ("zh", "core")
    return jax.shard_map(
        shards,
        mesh=fine,
        in_specs=(P(tok, hid), P(tok, hid), P(hid, tok), P(hid, tok)),
        out_specs=P(tok, hid),
        check_vma=False,
    )
```

```python
import functools
import math

import jax
import jax.numpy as jnp
from jax import lax
from jax.experimental import pallas as pl
from jax.experimental.pallas import tpu as pltpu
from jax.sharding import Mesh, PartitionSpec as P

RANK = 8
SEQ_LEN = 64
AXES = ("zl", "y", "x", "zh", "core")
SIZES = (4, 4, 4, 2, 2)
DEPTH = 1024
GROUPS = 4


def ring(x, axis, step):
    n = SIZES[AXES.index(axis)]
    return lax.ppermute(x, axis, [(i, (i + step) % n) for i in range(n)])


def flip(x, axis, mask):
    n = SIZES[AXES.index(axis)]
    return lax.ppermute(x, axis, [(i, i ^ mask) for i in range(n)])


def project_kernel(count, place_ref, *refs):
    rows_refs = refs[:count]
    grads_ref, acts_ref, keep_ref, send_ref, total_ref = refs[count:]
    tokens = grads_ref.shape[0]
    shape = (-1, GROUPS, RANK, tokens)
    start = 0
    for part, source in enumerate((grads_ref, acts_ref)):
        for at in range(0, source.shape[1], DEPTH):
            rows = jnp.concatenate([r[:, start : start + DEPTH] for r in rows_refs], axis=0)
            product = lax.dot_general(
                rows,
                source[:, at : at + DEPTH],
                (((1,), (1,)), ((), ())),
                preferred_element_type=jnp.float32,
            ).reshape(shape)
            total_ref[part] = product if at == 0 else total_ref[part] + product
            start += DEPTH
    base = place_ref[0]
    for other in range(2):
        mine = base ^ (2 * other)
        keep_ref[other] = total_ref[:, :, mine]
        send_ref[other] = total_ref[:, :, mine ^ 1]


def project(blocks, grads, acts, place):
    tokens, features = grads.shape[0], grads.shape[1] + acts.shape[1]
    rows = sum(b.shape[0] for b in blocks)
    parts = rows // (GROUPS * RANK)
    half = jax.ShapeDtypeStruct((2, 2, parts, RANK, tokens), jnp.float32)
    vmem = pl.BlockSpec(memory_space=pltpu.VMEM)
    return pl.pallas_call(
        functools.partial(project_kernel, len(blocks)),
        out_shape=(half, half),
        in_specs=[pl.BlockSpec(memory_space=pltpu.SMEM)] + [vmem] * (len(blocks) + 2),
        out_specs=(vmem, vmem),
        scratch_shapes=[pltpu.VMEM((2, parts, GROUPS, RANK, tokens), jnp.float32)],
        compiler_params=pltpu.CompilerParams(vmem_limit_bytes=VMEM_LIMIT),
        cost_estimate=pl.CostEstimate(flops=1 << 20, bytes_accessed=1 << 16, transcendentals=0),
    )(place, *blocks, grads, acts)


VMEM_LIMIT = 12 << 20


def finish_kernel(place_ref, sums1_ref, sums2_ref, sums3_ref, kept_ref, got_ref, back_ref, out_ref):
    y, x = place_ref[1], place_ref[2]
    total = kept_ref[0] + got_ref[0] + back_ref[...]
    sums4 = (total[0] * total[1]).sum(axis=1)
    sums = jnp.concatenate([sums1_ref[...], sums2_ref[...], sums3_ref[...], sums4], axis=0)
    seqs, tokens = out_ref.shape[0], sums.shape[1]
    row = lax.broadcasted_iota(jnp.int32, (seqs, tokens), 0)
    token = lax.broadcasted_iota(jnp.int32, (seqs, tokens), 1)
    ones = (row == token // SEQ_LEN).astype(jnp.float32)
    scores = lax.dot_general(
        ones,
        sums,
        (((1,), (1,)), ((), ())),
        precision=lax.Precision.HIGHEST,
        preferred_element_type=jnp.float32,
    )
    source = lax.broadcasted_iota(jnp.int32, (32, 32), 0)
    query = lax.broadcasted_iota(jnp.int32, (32, 32), 1)
    colour = query % 2
    off_y, off_x = (query // 8 - y) & 3, ((query // 2) % 4 - x) & 3

    def stands(off):
        return jnp.where(off == 3, 1, jnp.where(off == 0, 0, off + 1))

    first = stands(jnp.where(colour == 0, off_y, off_x))
    second = stands(jnp.where(colour == 0, off_x, off_y))
    wanted = colour * 4 + jnp.where(
        second == 0,
        first,
        jnp.where(second == 3, 24 + first, 8 + 8 * (first // 2) + 2 * (second - 1) + first % 2),
    )
    out = jnp.dot(
        scores,
        (source == wanted).astype(jnp.float32),
        precision=lax.Precision.HIGHEST,
        preferred_element_type=jnp.float32,
    )
    out_ref[...] = out * (1.0 / math.sqrt(SEQ_LEN * RANK))


def finish(place, sums, kept, got, back):
    vmem = pl.BlockSpec(memory_space=pltpu.VMEM)
    return pl.pallas_call(
        finish_kernel,
        out_shape=jax.ShapeDtypeStruct((8, 32), jnp.float32),
        in_specs=[pl.BlockSpec(memory_space=pltpu.SMEM)] + [vmem] * 6,
        out_specs=vmem,
        compiler_params=pltpu.CompilerParams(vmem_limit_bytes=4 << 20),
    )(place, *sums, kept, got, back)


def shards(train_grads, train_acts, out_factors, in_factors):
    zl, y, x, zh, core = (lax.axis_index(a) for a in AXES)
    place = jnp.stack([zl ^ (2 * zh + core), y, x])
    own = jnp.concatenate([out_factors.T, in_factors.T], axis=1)
    features = own.shape[1]
    with jax.named_scope("z_shifts"):
        stacked = jnp.stack([own] + [flip(own, "zl", k) for k in (1, 2, 3)])

    def first(rows, axis):
        block = rows.reshape(GROUPS * RANK, features)
        before, after, far = (ring(block, axis, step) for step in (1, -1, 2))
        return jnp.concatenate([block, before]), jnp.concatenate([after, far])

    def both(block, axis):
        return ring(block, axis, 1), ring(block, axis, -1)

    def exchange(sent):
        return lax.ppermute(sent, "zh", [(0, 1), (1, 0)])

    def over(send):
        return lax.ppermute(send, "core", [(0, 1), (1, 0)])

    def sums(keep, got, back):
        total = keep[0] + got[0] + back
        return (total[0] * total[1]).sum(axis=1)

    def work(blocks):
        keep, send = project(blocks, train_grads, train_acts, place)
        return keep, over(send)
    with jax.named_scope("first_axis"):
        lo_a, hi_a = first(stacked[:, :RANK], "y")
        lo_b, hi_b = first(stacked[:, RANK:], "x")
        lo_a, lo_b = lax.optimization_barrier((lo_a, lo_b))
        hi_a, hi_b = lax.optimization_barrier((hi_a, hi_b))
    with jax.named_scope("second_axis"):
        lo = both(lo_a, "x") + both(lo_b, "y")
    with jax.named_scope("reduce"):
        keep1, got1 = work((lo_a, hi_a, lo_b, hi_b))
        hi_a, hi_b, keep1 = lax.optimization_barrier((hi_a, hi_b, keep1))
        sums1 = sums(keep1, got1, exchange(keep1[1] + got1[1]))
        lo, keep1 = lax.optimization_barrier((lo, keep1))
    with jax.named_scope("second_axis"):
        hi = both(hi_a, "x") + both(hi_b, "y")
    with jax.named_scope("reduce"):
        keep2, got2 = work(lo)
        hi, (keep2, sums1) = lax.optimization_barrier((hi, (keep2, sums1)))
        sums2 = sums(keep2, got2, exchange(keep2[1] + got2[1]))
    with jax.named_scope("second_axis"):
        from_lo, from_hi = lax.optimization_barrier(((lo[0], lo[2]), (hi[1], hi[3])))
        far = (
            ring(from_lo[0], "x", 1),
            ring(from_hi[0], "x", -1),
            ring(from_lo[1], "y", 1),
            ring(from_hi[1], "y", -1),
        )
    with jax.named_scope("reduce"):
        keep3, got3 = work(hi)
        sent3 = keep3[1] + got3[1]
        back3 = exchange(sent3)
        far, sums2, sent3 = lax.optimization_barrier((far, sums2, sent3))
        keep4, got4 = work(far)
        sums3 = sums(keep3, got3, back3)
        back4 = exchange(keep4[1] + got4[1])
        return finish(place, (sums1, sums2, sums3), keep4, got4, back4)


def solution(mesh):
    fine = Mesh(mesh.devices.reshape(SIZES), AXES)
    tok, hid = ("zl", "y", "x"), ("zh", "core")
    return jax.shard_map(
        shards,
        mesh=fine,
        in_specs=(P(tok, hid), P(tok, hid), P(hid, tok), P(hid, tok)),
        out_specs=P(tok, hid),
        check_vma=False,
    )
```

```python
import functools
import math

import jax
import jax.numpy as jnp
from jax import lax
from jax.experimental import pallas as pl
from jax.experimental.pallas import tpu as pltpu
from jax.sharding import Mesh, PartitionSpec as P

RANK = 8
SEQ_LEN = 64
AXES = ("zl", "y", "x", "zh", "core")
SIZES = (4, 4, 4, 2, 2)
DEPTH = 1024
GROUPS = 4


def ring(x, axis, step):
    n = SIZES[AXES.index(axis)]
    return lax.ppermute(x, axis, [(i, (i + step) % n) for i in range(n)])


def flip(x, axis, mask):
    n = SIZES[AXES.index(axis)]
    return lax.ppermute(x, axis, [(i, i ^ mask) for i in range(n)])


def project_kernel(count, place_ref, *refs):
    rows_refs = refs[:count]
    grads_ref, acts_ref, keep_ref, send_ref, total_ref = refs[count:]
    tokens = grads_ref.shape[0]
    shape = (-1, GROUPS, RANK, tokens)
    start = 0
    for part, source in enumerate((grads_ref, acts_ref)):
        for at in range(0, source.shape[1], DEPTH):
            rows = jnp.concatenate([r[:, start : start + DEPTH] for r in rows_refs], axis=0)
            product = lax.dot_general(
                rows,
                source[:, at : at + DEPTH],
                (((1,), (1,)), ((), ())),
                preferred_element_type=jnp.float32,
            ).reshape(shape)
            total_ref[part] = product if at == 0 else total_ref[part] + product
            start += DEPTH
    base = place_ref[0]
    for other in range(2):
        mine = base ^ (2 * other)
        keep_ref[other] = total_ref[:, :, mine]
        send_ref[other] = total_ref[:, :, mine ^ 1]


def project(blocks, grads, acts, place):
    tokens, features = grads.shape[0], grads.shape[1] + acts.shape[1]
    rows = sum(b.shape[0] for b in blocks)
    parts = rows // (GROUPS * RANK)
    half = jax.ShapeDtypeStruct((2, 2, parts, RANK, tokens), jnp.float32)
    vmem = pl.BlockSpec(memory_space=pltpu.VMEM)
    return pl.pallas_call(
        functools.partial(project_kernel, len(blocks)),
        out_shape=(half, half),
        in_specs=[pl.BlockSpec(memory_space=pltpu.SMEM)] + [vmem] * (len(blocks) + 2),
        out_specs=(vmem, vmem),
        scratch_shapes=[pltpu.VMEM((2, parts, GROUPS, RANK, tokens), jnp.float32)],
        compiler_params=pltpu.CompilerParams(vmem_limit_bytes=VMEM_LIMIT),
        cost_estimate=pl.CostEstimate(flops=1 << 20, bytes_accessed=1 << 16, transcendentals=0),
    )(place, *blocks, grads, acts)


VMEM_LIMIT = 12 << 20


def finish_kernel(place_ref, sums1_ref, sums2_ref, sums3_ref, kept_ref, got_ref, back_ref, out_ref):
    y, x = place_ref[1], place_ref[2]
    total = kept_ref[0] + got_ref[0] + back_ref[...]
    sums4 = (total[0] * total[1]).sum(axis=1)
    sums = jnp.concatenate([sums1_ref[...], sums2_ref[...], sums3_ref[...], sums4], axis=0)
    seqs, tokens = out_ref.shape[0], sums.shape[1]
    row = lax.broadcasted_iota(jnp.int32, (seqs, tokens), 0)
    token = lax.broadcasted_iota(jnp.int32, (seqs, tokens), 1)
    ones = (row == token // SEQ_LEN).astype(jnp.float32)
    scores = lax.dot_general(
        ones,
        sums,
        (((1,), (1,)), ((), ())),
        precision=lax.Precision.HIGHEST,
        preferred_element_type=jnp.float32,
    )
    source = lax.broadcasted_iota(jnp.int32, (32, 32), 0)
    query = lax.broadcasted_iota(jnp.int32, (32, 32), 1)
    colour = query % 2
    off_y, off_x = (query // 8 - y) & 3, ((query // 2) % 4 - x) & 3

    def stands(off):
        return jnp.where(off == 3, 1, jnp.where(off == 0, 0, off + 1))

    first = stands(jnp.where(colour == 0, off_y, off_x))
    second = stands(jnp.where(colour == 0, off_x, off_y))
    wanted = colour * 4 + jnp.where(
        second == 0,
        first,
        jnp.where(second == 3, 24 + first, 8 + 8 * (first // 2) + 2 * (second - 1) + first % 2),
    )
    out = jnp.dot(
        scores,
        (source == wanted).astype(jnp.float32),
        precision=lax.Precision.HIGHEST,
        preferred_element_type=jnp.float32,
    )
    out_ref[...] = out * (1.0 / math.sqrt(SEQ_LEN * RANK))


def finish(place, sums, kept, got, back):
    vmem = pl.BlockSpec(memory_space=pltpu.VMEM)
    return pl.pallas_call(
        finish_kernel,
        out_shape=jax.ShapeDtypeStruct((8, 32), jnp.float32),
        in_specs=[pl.BlockSpec(memory_space=pltpu.SMEM)] + [vmem] * 6,
        out_specs=vmem,
        compiler_params=pltpu.CompilerParams(vmem_limit_bytes=4 << 20),
    )(place, *sums, kept, got, back)


def shards(train_grads, train_acts, out_factors, in_factors):
    zl, y, x, zh, core = (lax.axis_index(a) for a in AXES)
    place = jnp.stack([zl ^ (2 * zh + core), y, x])
    own = jnp.concatenate([out_factors.T, in_factors.T], axis=1)
    features = own.shape[1]
    with jax.named_scope("z_shifts"):
        stacked = jnp.stack([own] + [flip(own, "zl", k) for k in (1, 2, 3)])

    def first(rows, axis):
        block = rows.reshape(GROUPS * RANK, features)
        half = block.shape[0] // 2
        before, after = ring(block, axis, 1), ring(block, axis, -1)
        far = ring(before[:half], axis, 1), ring(after[half:], axis, -1)
        return jnp.concatenate([block, before]), jnp.concatenate([after, *far])

    def both(block, axis):
        return ring(block, axis, 1), ring(block, axis, -1)

    def exchange(sent):
        return lax.ppermute(sent, "zh", [(0, 1), (1, 0)])

    def over(send):
        return lax.ppermute(send, "core", [(0, 1), (1, 0)])

    def sums(keep, got, back):
        total = keep[0] + got[0] + back
        return (total[0] * total[1]).sum(axis=1)

    def work(blocks):
        keep, send = project(blocks, train_grads, train_acts, place)
        return keep, over(send)
    with jax.named_scope("first_axis"):
        lo_a, hi_a = first(stacked[:, :RANK], "y")
        lo_b, hi_b = first(stacked[:, RANK:], "x")
        lo_a, lo_b = lax.optimization_barrier((lo_a, lo_b))
        hi_a, hi_b = lax.optimization_barrier((hi_a, hi_b))
    with jax.named_scope("second_axis"):
        lo = both(lo_a, "x") + both(lo_b, "y")
    with jax.named_scope("reduce"):
        keep1, got1 = work((lo_a, hi_a, lo_b, hi_b))
        hi_a, hi_b, keep1 = lax.optimization_barrier((hi_a, hi_b, keep1))
        sums1 = sums(keep1, got1, exchange(keep1[1] + got1[1]))
        lo, keep1 = lax.optimization_barrier((lo, keep1))
    with jax.named_scope("second_axis"):
        hi = both(hi_a, "x") + both(hi_b, "y")
    with jax.named_scope("reduce"):
        keep2, got2 = work(lo)
        hi, (keep2, sums1) = lax.optimization_barrier((hi, (keep2, sums1)))
        sums2 = sums(keep2, got2, exchange(keep2[1] + got2[1]))
    with jax.named_scope("second_axis"):
        from_lo, from_hi = lax.optimization_barrier(((lo[0], lo[2]), (hi[1], hi[3])))
        far = (
            ring(from_lo[0], "x", 1),
            ring(from_hi[0], "x", -1),
            ring(from_lo[1], "y", 1),
            ring(from_hi[1], "y", -1),
        )
    with jax.named_scope("reduce"):
        keep3, got3 = work(hi)
        sent3 = keep3[1] + got3[1]
        back3 = exchange(sent3)
        far, sums2, sent3 = lax.optimization_barrier((far, sums2, sent3))
        keep4, got4 = work(far)
        sums3 = sums(keep3, got3, back3)
        sent4, sums3 = lax.optimization_barrier((keep4[1] + got4[1], sums3))
        back4 = exchange(sent4)
        return finish(place, (sums1, sums2, sums3), keep4, got4, back4)


def solution(mesh):
    fine = Mesh(mesh.devices.reshape(SIZES), AXES)
    tok, hid = ("zl", "y", "x"), ("zh", "core")
    return jax.shard_map(
        shards,
        mesh=fine,
        in_specs=(P(tok, hid), P(tok, hid), P(hid, tok), P(hid, tok)),
        out_specs=P(tok, hid),
        check_vma=False,
    )
```

```python
import functools
import math

import jax
import jax.numpy as jnp
from jax import lax
from jax.experimental import pallas as pl
from jax.experimental.pallas import tpu as pltpu
from jax.sharding import Mesh, PartitionSpec as P

RANK = 8
SEQ_LEN = 64
AXES = ("zl", "y", "x", "zh", "core")
SIZES = (4, 4, 4, 2, 2)
DEPTH = 1024
GROUPS = 4


def ring(x, axis, step):
    n = SIZES[AXES.index(axis)]
    return lax.ppermute(x, axis, [(i, (i + step) % n) for i in range(n)])


def flip(x, axis, mask):
    n = SIZES[AXES.index(axis)]
    return lax.ppermute(x, axis, [(i, i ^ mask) for i in range(n)])


def project_kernel(count, place_ref, *refs):
    rows_refs = refs[:count]
    grads_ref, acts_ref, keep_ref, send_ref, total_ref = refs[count:]
    tokens = grads_ref.shape[0]
    shape = (-1, GROUPS, RANK, tokens)
    start = 0
    for part, source in enumerate((grads_ref, acts_ref)):
        for at in range(0, source.shape[1], DEPTH):
            rows = jnp.concatenate([r[:, start : start + DEPTH] for r in rows_refs], axis=0)
            product = lax.dot_general(
                rows,
                source[:, at : at + DEPTH],
                (((1,), (1,)), ((), ())),
                preferred_element_type=jnp.float32,
            ).reshape(shape)
            total_ref[part] = product if at == 0 else total_ref[part] + product
            start += DEPTH
    base = place_ref[0]
    for other in range(2):
        mine = base ^ (2 * other)
        keep_ref[other] = total_ref[:, :, mine]
        send_ref[other] = total_ref[:, :, mine ^ 1]


def project(blocks, grads, acts, place):
    tokens, features = grads.shape[0], grads.shape[1] + acts.shape[1]
    rows = sum(b.shape[0] for b in blocks)
    parts = rows // (GROUPS * RANK)
    half = jax.ShapeDtypeStruct((2, 2, parts, RANK, tokens), jnp.float32)
    vmem = pl.BlockSpec(memory_space=pltpu.VMEM)
    return pl.pallas_call(
        functools.partial(project_kernel, len(blocks)),
        out_shape=(half, half),
        in_specs=[pl.BlockSpec(memory_space=pltpu.SMEM)] + [vmem] * (len(blocks) + 2),
        out_specs=(vmem, vmem),
        scratch_shapes=[pltpu.VMEM((2, parts, GROUPS, RANK, tokens), jnp.float32)],
        compiler_params=pltpu.CompilerParams(vmem_limit_bytes=VMEM_LIMIT),
        cost_estimate=pl.CostEstimate(flops=1 << 20, bytes_accessed=1 << 16, transcendentals=0),
    )(place, *blocks, grads, acts)


VMEM_LIMIT = 12 << 20


def finish_kernel(place_ref, sums1_ref, sums2_ref, sums3_ref, kept_ref, got_ref, back_ref, out_ref):
    y, x = place_ref[1], place_ref[2]
    total = kept_ref[0] + got_ref[0] + back_ref[...]
    sums4 = (total[0] * total[1]).sum(axis=1)
    sums = jnp.concatenate([sums1_ref[...], sums2_ref[...], sums3_ref[...], sums4], axis=0)
    seqs, tokens = out_ref.shape[0], sums.shape[1]
    row = lax.broadcasted_iota(jnp.int32, (seqs, tokens), 0)
    token = lax.broadcasted_iota(jnp.int32, (seqs, tokens), 1)
    ones = (row == token // SEQ_LEN).astype(jnp.float32)
    scores = lax.dot_general(
        ones,
        sums,
        (((1,), (1,)), ((), ())),
        precision=lax.Precision.HIGHEST,
        preferred_element_type=jnp.float32,
    )
    source = lax.broadcasted_iota(jnp.int32, (32, 32), 0)
    query = lax.broadcasted_iota(jnp.int32, (32, 32), 1)
    colour = query % 2
    off_y, off_x = (query // 8 - y) & 3, ((query // 2) % 4 - x) & 3

    def stands(off):
        return jnp.where(off == 3, 1, jnp.where(off == 0, 0, off + 1))

    first = stands(jnp.where(colour == 0, off_y, off_x))
    second = stands(jnp.where(colour == 0, off_x, off_y))
    wanted = colour * 4 + jnp.where(
        second == 0,
        first,
        jnp.where(second == 3, 24 + first, 8 + 8 * (first // 2) + 2 * (second - 1) + first % 2),
    )
    out = jnp.dot(
        scores,
        (source == wanted).astype(jnp.float32),
        precision=lax.Precision.HIGHEST,
        preferred_element_type=jnp.float32,
    )
    out_ref[...] = out * (1.0 / math.sqrt(SEQ_LEN * RANK))


def finish(place, sums, kept, got, back):
    vmem = pl.BlockSpec(memory_space=pltpu.VMEM)
    return pl.pallas_call(
        finish_kernel,
        out_shape=jax.ShapeDtypeStruct((8, 32), jnp.float32),
        in_specs=[pl.BlockSpec(memory_space=pltpu.SMEM)] + [vmem] * 6,
        out_specs=vmem,
        compiler_params=pltpu.CompilerParams(vmem_limit_bytes=4 << 20),
    )(place, *sums, kept, got, back)


def shards(train_grads, train_acts, out_factors, in_factors):
    zl, y, x, zh, core = (lax.axis_index(a) for a in AXES)
    place = jnp.stack([zl ^ (2 * zh + core), y, x])
    own = jnp.concatenate([out_factors.T, in_factors.T], axis=1)
    features = own.shape[1]
    with jax.named_scope("z_shifts"):
        stacked = jnp.stack([own] + [flip(own, "zl", k) for k in (1, 2, 3)])

    def first(rows, axis, direct):
        block = rows.reshape(GROUPS * RANK, features)
        half = block.shape[0] // 2
        before, after = ring(block, axis, 1), ring(block, axis, -1)
        if direct:
            far = (ring(block, axis, 2),)
        else:
            far = ring(before[:half], axis, 1), ring(after[half:], axis, -1)
        return jnp.concatenate([block, before]), jnp.concatenate([after, *far])

    def both(block, axis):
        return ring(block, axis, 1), ring(block, axis, -1)

    def exchange(sent):
        return lax.ppermute(sent, "zh", [(0, 1), (1, 0)])

    def over(send):
        return lax.ppermute(send, "core", [(0, 1), (1, 0)])

    def sums(keep, got, back):
        total = keep[0] + got[0] + back
        return (total[0] * total[1]).sum(axis=1)

    def work(blocks):
        keep, send = project(blocks, train_grads, train_acts, place)
        return keep, over(send)
    with jax.named_scope("first_axis"):
        lo_a, hi_a = first(stacked[:, :RANK], "y", True)
        lo_b, hi_b = first(stacked[:, RANK:], "x", False)
        hi_a, hi_b = lax.optimization_barrier((hi_a, hi_b))
    with jax.named_scope("second_axis"):
        lo = both(lo_a, "x") + both(lo_b, "y")
    with jax.named_scope("reduce"):
        keep1, got1 = work((lo_a, hi_a, lo_b, hi_b))
        hi_a, hi_b, keep1 = lax.optimization_barrier((hi_a, hi_b, keep1))
        sums1 = sums(keep1, got1, exchange(keep1[1] + got1[1]))
        lo, keep1 = lax.optimization_barrier((lo, keep1))
    with jax.named_scope("second_axis"):
        hi = both(hi_a, "x") + both(hi_b, "y")
    with jax.named_scope("reduce"):
        keep2, got2 = work(lo)
        hi, (keep2, sums1) = lax.optimization_barrier((hi, (keep2, sums1)))
        sums2 = sums(keep2, got2, exchange(keep2[1] + got2[1]))
    with jax.named_scope("second_axis"):
        from_lo, from_hi = lax.optimization_barrier(((lo[0], lo[2]), (hi[1], hi[3])))
        far = (
            ring(from_lo[0], "x", 1),
            ring(from_hi[0], "x", -1),
            ring(from_lo[1], "y", 1),
            ring(from_hi[1], "y", -1),
        )
    with jax.named_scope("reduce"):
        keep3, got3 = work(hi)
        sent3 = keep3[1] + got3[1]
        back3 = exchange(sent3)
        far, sums2, sent3 = lax.optimization_barrier((far, sums2, sent3))
        keep4, got4 = work(far)
        sums3 = sums(keep3, got3, back3)
        sent4, sums3 = lax.optimization_barrier((keep4[1] + got4[1], sums3))
        back4 = exchange(sent4)
        return finish(place, (sums1, sums2, sums3), keep4, got4, back4)


def solution(mesh):
    fine = Mesh(mesh.devices.reshape(SIZES), AXES)
    tok, hid = ("zl", "y", "x"), ("zh", "core")
    return jax.shard_map(
        shards,
        mesh=fine,
        in_specs=(P(tok, hid), P(tok, hid), P(hid, tok), P(hid, tok)),
        out_specs=P(tok, hid),
        check_vma=False,
    )
```

```python
import functools
import math

import jax
import jax.numpy as jnp
from jax import lax
from jax.experimental import pallas as pl
from jax.experimental.pallas import tpu as pltpu
from jax.sharding import Mesh, PartitionSpec as P

RANK = 8
SEQ_LEN = 64
AXES = ("zl", "y", "x", "zh", "core")
SIZES = (4, 4, 4, 2, 2)
DEPTH = 1024
GROUPS = 4


def ring(x, axis, step):
    n = SIZES[AXES.index(axis)]
    return lax.ppermute(x, axis, [(i, (i + step) % n) for i in range(n)])


def flip(x, axis, mask):
    n = SIZES[AXES.index(axis)]
    return lax.ppermute(x, axis, [(i, i ^ mask) for i in range(n)])


def project_kernel(count, place_ref, *refs):
    rows_refs = refs[:count]
    grads_ref, acts_ref, keep_ref, send_ref, total_ref = refs[count:]
    tokens = grads_ref.shape[0]
    shape = (-1, GROUPS, RANK, tokens)
    start = 0
    for part, source in enumerate((grads_ref, acts_ref)):
        for at in range(0, source.shape[1], DEPTH):
            rows = jnp.concatenate([r[:, start : start + DEPTH] for r in rows_refs], axis=0)
            product = lax.dot_general(
                rows,
                source[:, at : at + DEPTH],
                (((1,), (1,)), ((), ())),
                preferred_element_type=jnp.float32,
            ).reshape(shape)
            total_ref[part] = product if at == 0 else total_ref[part] + product
            start += DEPTH
    base = place_ref[0]
    for other in range(2):
        mine = base ^ (2 * other)
        keep_ref[other] = total_ref[:, :, mine]
        send_ref[other] = total_ref[:, :, mine ^ 1]


def project(blocks, grads, acts, place):
    tokens, features = grads.shape[0], grads.shape[1] + acts.shape[1]
    rows = sum(b.shape[0] for b in blocks)
    parts = rows // (GROUPS * RANK)
    half = jax.ShapeDtypeStruct((2, 2, parts, RANK, tokens), jnp.float32)
    vmem = pl.BlockSpec(memory_space=pltpu.VMEM)
    return pl.pallas_call(
        functools.partial(project_kernel, len(blocks)),
        out_shape=(half, half),
        in_specs=[pl.BlockSpec(memory_space=pltpu.SMEM)] + [vmem] * (len(blocks) + 2),
        out_specs=(vmem, vmem),
        scratch_shapes=[pltpu.VMEM((2, parts, GROUPS, RANK, tokens), jnp.float32)],
        compiler_params=pltpu.CompilerParams(vmem_limit_bytes=VMEM_LIMIT),
        cost_estimate=pl.CostEstimate(flops=1 << 20, bytes_accessed=1 << 16, transcendentals=0),
    )(place, *blocks, grads, acts)


VMEM_LIMIT = 12 << 20


def finish_kernel(place_ref, sums1_ref, sums2_ref, sums3_ref, kept_ref, got_ref, back_ref, out_ref):
    y, x = place_ref[1], place_ref[2]
    total = kept_ref[0] + got_ref[0] + back_ref[...]
    sums4 = (total[0] * total[1]).sum(axis=1)
    sums = jnp.concatenate([sums1_ref[...], sums2_ref[...], sums3_ref[...], sums4], axis=0)
    seqs, tokens = out_ref.shape[0], sums.shape[1]
    row = lax.broadcasted_iota(jnp.int32, (seqs, tokens), 0)
    token = lax.broadcasted_iota(jnp.int32, (seqs, tokens), 1)
    ones = (row == token // SEQ_LEN).astype(jnp.float32)
    scores = lax.dot_general(
        ones,
        sums,
        (((1,), (1,)), ((), ())),
        precision=lax.Precision.HIGHEST,
        preferred_element_type=jnp.float32,
    )
    source = lax.broadcasted_iota(jnp.int32, (32, 32), 0)
    query = lax.broadcasted_iota(jnp.int32, (32, 32), 1)
    colour = query % 2
    off_y, off_x = (query // 8 - y) & 3, ((query // 2) % 4 - x) & 3

    def stands(off):
        return jnp.where(off == 3, 1, jnp.where(off == 0, 0, off + 1))

    first = stands(jnp.where(colour == 0, off_y, off_x))
    second = stands(jnp.where(colour == 0, off_x, off_y))
    wanted = colour * 4 + jnp.where(
        second == 0,
        first,
        jnp.where(second == 3, 24 + first, 8 + 8 * (first // 2) + 2 * (second - 1) + first % 2),
    )
    out = jnp.dot(
        scores,
        (source == wanted).astype(jnp.float32),
        precision=lax.Precision.HIGHEST,
        preferred_element_type=jnp.float32,
    )
    out_ref[...] = out * (1.0 / math.sqrt(SEQ_LEN * RANK))


def finish(place, sums, kept, got, back):
    vmem = pl.BlockSpec(memory_space=pltpu.VMEM)
    return pl.pallas_call(
        finish_kernel,
        out_shape=jax.ShapeDtypeStruct((8, 32), jnp.float32),
        in_specs=[pl.BlockSpec(memory_space=pltpu.SMEM)] + [vmem] * 6,
        out_specs=vmem,
        compiler_params=pltpu.CompilerParams(vmem_limit_bytes=4 << 20),
    )(place, *sums, kept, got, back)


def shards(train_grads, train_acts, out_factors, in_factors):
    zl, y, x, zh, core = (lax.axis_index(a) for a in AXES)
    place = jnp.stack([zl ^ (2 * zh + core), y, x])
    own = jnp.concatenate([out_factors.T, in_factors.T], axis=1)
    features = own.shape[1]
    with jax.named_scope("z_shifts"):
        stacked = jnp.stack([own] + [flip(own, "zl", k) for k in (1, 2, 3)])

    def first(rows, axis):
        block = rows.reshape(GROUPS * RANK, features)
        half = block.shape[0] // 2
        before, after = ring(block, axis, 1), ring(block, axis, -1)
        far = ring(before[:half], axis, 1), ring(after[half:], axis, -1)
        return jnp.concatenate([block, before]), jnp.concatenate([after, *far])

    def both(block, axis):
        return ring(block, axis, 1), ring(block, axis, -1)

    def exchange(sent):
        return lax.ppermute(sent, "zh", [(0, 1), (1, 0)])

    def over(send):
        return lax.ppermute(send, "core", [(0, 1), (1, 0)])

    def sums(keep, got, back):
        total = keep[0] + got[0] + back
        return (total[0] * total[1]).sum(axis=1)

    def work(blocks):
        keep, send = project(blocks, train_grads, train_acts, place)
        return keep, over(send)
    with jax.named_scope("first_axis"):
        lo_a, hi_a = first(stacked[:, :RANK], "y")
        lo_b, hi_b = first(stacked[:, RANK:], "x")
        lo_a, lo_b, hi_b = lax.optimization_barrier((lo_a, lo_b, hi_b))
        hi_a, hi_b = lax.optimization_barrier((hi_a, hi_b))
    with jax.named_scope("second_axis"):
        lo = both(lo_a, "x") + both(lo_b, "y")
    with jax.named_scope("reduce"):
        keep1, got1 = work((lo_a, hi_a, lo_b, hi_b))
        hi_a, hi_b, keep1 = lax.optimization_barrier((hi_a, hi_b, keep1))
        sums1 = sums(keep1, got1, exchange(keep1[1] + got1[1]))
        lo, keep1 = lax.optimization_barrier((lo, keep1))
    with jax.named_scope("second_axis"):
        hi = both(hi_a, "x") + both(hi_b, "y")
    with jax.named_scope("reduce"):
        keep2, got2 = work(lo)
        hi, (keep2, sums1) = lax.optimization_barrier((hi, (keep2, sums1)))
        sums2 = sums(keep2, got2, exchange(keep2[1] + got2[1]))
    with jax.named_scope("second_axis"):
        from_lo, from_hi = lax.optimization_barrier(((lo[0], lo[2]), (hi[1], hi[3])))
        far = (
            ring(from_lo[0], "x", 1),
            ring(from_hi[0], "x", -1),
            ring(from_lo[1], "y", 1),
            ring(from_hi[1], "y", -1),
        )
    with jax.named_scope("reduce"):
        keep3, got3 = work(hi)
        sent3 = keep3[1] + got3[1]
        back3 = exchange(sent3)
        far, sums2, sent3 = lax.optimization_barrier((far, sums2, sent3))
        keep4, got4 = work(far)
        sums3 = sums(keep3, got3, back3)
        sent4, sums3 = lax.optimization_barrier((keep4[1] + got4[1], sums3))
        back4 = exchange(sent4)
        return finish(place, (sums1, sums2, sums3), keep4, got4, back4)


def solution(mesh):
    fine = Mesh(mesh.devices.reshape(SIZES), AXES)
    tok, hid = ("zl", "y", "x"), ("zh", "core")
    return jax.shard_map(
        shards,
        mesh=fine,
        in_specs=(P(tok, hid), P(tok, hid), P(hid, tok), P(hid, tok)),
        out_specs=P(tok, hid),
        check_vma=False,
    )
```

```python
import functools
import math

import jax
import jax.numpy as jnp
from jax import lax
from jax.experimental import pallas as pl
from jax.experimental.pallas import tpu as pltpu
from jax.sharding import Mesh, PartitionSpec as P

RANK = 8
SEQ_LEN = 64
AXES = ("zl", "y", "x", "zh", "core")
SIZES = (4, 4, 4, 2, 2)
DEPTH = 1024
GROUPS = 4


def ring(x, axis, step):
    n = SIZES[AXES.index(axis)]
    return lax.ppermute(x, axis, [(i, (i + step) % n) for i in range(n)])


def flip(x, axis, mask):
    n = SIZES[AXES.index(axis)]
    return lax.ppermute(x, axis, [(i, i ^ mask) for i in range(n)])


def project_kernel(count, place_ref, *refs):
    rows_refs = refs[:count]
    grads_ref, acts_ref, keep_ref, send_ref, total_ref = refs[count:]
    tokens = grads_ref.shape[0]
    shape = (-1, GROUPS, RANK, tokens)
    start = 0
    for part, source in enumerate((grads_ref, acts_ref)):
        for at in range(0, source.shape[1], DEPTH):
            rows = jnp.concatenate([r[:, start : start + DEPTH] for r in rows_refs], axis=0)
            product = lax.dot_general(
                rows,
                source[:, at : at + DEPTH],
                (((1,), (1,)), ((), ())),
                preferred_element_type=jnp.float32,
            ).reshape(shape)
            total_ref[part] = product if at == 0 else total_ref[part] + product
            start += DEPTH
    base = place_ref[0]
    for other in range(2):
        mine = base ^ (2 * other)
        keep_ref[other] = total_ref[:, :, mine]
        send_ref[other] = total_ref[:, :, mine ^ 1]


def project(blocks, grads, acts, place):
    tokens, features = grads.shape[0], grads.shape[1] + acts.shape[1]
    rows = sum(b.shape[0] for b in blocks)
    parts = rows // (GROUPS * RANK)
    half = jax.ShapeDtypeStruct((2, 2, parts, RANK, tokens), jnp.float32)
    vmem = pl.BlockSpec(memory_space=pltpu.VMEM)
    return pl.pallas_call(
        functools.partial(project_kernel, len(blocks)),
        out_shape=(half, half),
        in_specs=[pl.BlockSpec(memory_space=pltpu.SMEM)] + [vmem] * (len(blocks) + 2),
        out_specs=(vmem, vmem),
        scratch_shapes=[pltpu.VMEM((2, parts, GROUPS, RANK, tokens), jnp.float32)],
        compiler_params=pltpu.CompilerParams(vmem_limit_bytes=VMEM_LIMIT),
        cost_estimate=pl.CostEstimate(flops=1 << 20, bytes_accessed=1 << 16, transcendentals=0),
    )(place, *blocks, grads, acts)


VMEM_LIMIT = 12 << 20


def finish_kernel(place_ref, sums1_ref, sums2_ref, sums3_ref, kept_ref, got_ref, back_ref, out_ref):
    y, x = place_ref[1], place_ref[2]
    total = kept_ref[0] + got_ref[0] + back_ref[...]
    sums4 = (total[0] * total[1]).sum(axis=1)
    sums = jnp.concatenate([sums1_ref[...], sums2_ref[...], sums3_ref[...], sums4], axis=0)
    seqs, tokens = out_ref.shape[0], sums.shape[1]
    row = lax.broadcasted_iota(jnp.int32, (seqs, tokens), 0)
    token = lax.broadcasted_iota(jnp.int32, (seqs, tokens), 1)
    ones = (row == token // SEQ_LEN).astype(jnp.float32)
    scores = lax.dot_general(
        ones,
        sums,
        (((1,), (1,)), ((), ())),
        precision=lax.Precision.HIGHEST,
        preferred_element_type=jnp.float32,
    )
    source = lax.broadcasted_iota(jnp.int32, (32, 32), 0)
    query = lax.broadcasted_iota(jnp.int32, (32, 32), 1)
    colour = query % 2
    off_y, off_x = (query // 8 - y) & 3, ((query // 2) % 4 - x) & 3

    def stands(off):
        return jnp.where(off == 3, 1, jnp.where(off == 0, 0, off + 1))

    first = stands(jnp.where(colour == 0, off_y, off_x))
    second = stands(jnp.where(colour == 0, off_x, off_y))
    wanted = colour * 4 + jnp.where(
        second == 0,
        first,
        jnp.where(second == 3, 24 + first, 8 + 8 * (first // 2) + 2 * (second - 1) + first % 2),
    )
    out = jnp.dot(
        scores,
        (source == wanted).astype(jnp.float32),
        precision=lax.Precision.HIGHEST,
        preferred_element_type=jnp.float32,
    )
    out_ref[...] = out * (1.0 / math.sqrt(SEQ_LEN * RANK))


def finish(place, sums, kept, got, back):
    vmem = pl.BlockSpec(memory_space=pltpu.VMEM)
    return pl.pallas_call(
        finish_kernel,
        out_shape=jax.ShapeDtypeStruct((8, 32), jnp.float32),
        in_specs=[pl.BlockSpec(memory_space=pltpu.SMEM)] + [vmem] * 6,
        out_specs=vmem,
        compiler_params=pltpu.CompilerParams(vmem_limit_bytes=4 << 20),
    )(place, *sums, kept, got, back)


def shards(train_grads, train_acts, out_factors, in_factors):
    zl, y, x, zh, core = (lax.axis_index(a) for a in AXES)
    place = jnp.stack([zl ^ (2 * zh + core), y, x])
    own = jnp.concatenate([out_factors.T, in_factors.T], axis=1)
    features = own.shape[1]
    with jax.named_scope("z_shifts"):
        stacked = jnp.stack([own] + [flip(own, "zl", k) for k in (1, 2, 3)])

    def first(rows, axis):
        block = rows.reshape(GROUPS * RANK, features)
        half = block.shape[0] // 2
        before, after = ring(block, axis, 1), ring(block, axis, -1)
        return jnp.concatenate([block, before]), after, before[:half], after[half:]

    def both(block, axis):
        return ring(block, axis, 1), ring(block, axis, -1)

    def exchange(sent):
        return lax.ppermute(sent, "zh", [(0, 1), (1, 0)])

    def over(send):
        return lax.ppermute(send, "core", [(0, 1), (1, 0)])

    def sums(keep, got, back):
        total = keep[0] + got[0] + back
        return (total[0] * total[1]).sum(axis=1)

    def work(blocks):
        keep, send = project(blocks, train_grads, train_acts, place)
        return keep, over(send)
    with jax.named_scope("first_axis"):
        (lo_a, after_a, up_a, down_a), (lo_b, after_b, up_b, down_b) = lax.optimization_barrier(
            (first(stacked[:, :RANK], "y"), first(stacked[:, RANK:], "x"))
        )
        hi_a = jnp.concatenate([after_a, ring(up_a, "y", 1), ring(down_a, "y", -1)])
        hi_b = jnp.concatenate([after_b, ring(up_b, "x", 1), ring(down_b, "x", -1)])
        hi_a, hi_b = lax.optimization_barrier((hi_a, hi_b))
    with jax.named_scope("second_axis"):
        lo = both(lo_a, "x") + both(lo_b, "y")
    with jax.named_scope("reduce"):
        keep1, got1 = work((lo_a, hi_a, lo_b, hi_b))
        hi_a, hi_b, keep1 = lax.optimization_barrier((hi_a, hi_b, keep1))
        sums1 = sums(keep1, got1, exchange(keep1[1] + got1[1]))
        lo, keep1 = lax.optimization_barrier((lo, keep1))
    with jax.named_scope("second_axis"):
        hi = both(hi_a, "x") + both(hi_b, "y")
    with jax.named_scope("reduce"):
        keep2, got2 = work(lo)
        hi, (keep2, sums1) = lax.optimization_barrier((hi, (keep2, sums1)))
        sums2 = sums(keep2, got2, exchange(keep2[1] + got2[1]))
    with jax.named_scope("second_axis"):
        from_lo, from_hi = lax.optimization_barrier(((lo[0], lo[2]), (hi[1], hi[3])))
        far = (
            ring(from_lo[0], "x", 1),
            ring(from_hi[0], "x", -1),
            ring(from_lo[1], "y", 1),
            ring(from_hi[1], "y", -1),
        )
    with jax.named_scope("reduce"):
        keep3, got3 = work(hi)
        sent3 = keep3[1] + got3[1]
        back3 = exchange(sent3)
        far, sums2, sent3 = lax.optimization_barrier((far, sums2, sent3))
        keep4, got4 = work(far)
        sums3 = sums(keep3, got3, back3)
        sent4, sums3 = lax.optimization_barrier((keep4[1] + got4[1], sums3))
        back4 = exchange(sent4)
        return finish(place, (sums1, sums2, sums3), keep4, got4, back4)


def solution(mesh):
    fine = Mesh(mesh.devices.reshape(SIZES), AXES)
    tok, hid = ("zl", "y", "x"), ("zh", "core")
    return jax.shard_map(
        shards,
        mesh=fine,
        in_specs=(P(tok, hid), P(tok, hid), P(hid, tok), P(hid, tok)),
        out_specs=P(tok, hid),
        check_vma=False,
    )
```
